512 devices in a mesh: leaf: 128 (over z, y, core), sub: 4 (over x).
Axes of the slice: x: 4, y: 8, z: 8, core: 2. Of those that a mesh axis runs over, the one named last changes fastest.
Arguments:
- density: bfloat16 [2, 128, 524288], P(None, None, ('leaf', 'sub')), may hold values from -6 to 6
- coords: bfloat16 [3, 524288], P(None, ('leaf', 'sub')), may hold values from -3 to 3
- weights: bfloat16 [524288], P(('leaf', 'sub')), may hold values from 0.033935547 to 0.33984375
- counts: int32 [4096], P(('leaf', 'sub')), may hold values from 1 to 27, as said below
- neighbors: int32 [4096, 27], P(('leaf', 'sub')), may hold values from 0 to 11, as said below
- skeleton: int32 [512, 128], P(('leaf', 'sub')), may hold values from 0 to 1023
- compress: bfloat16 [2, 128, 524288], P(None, None, ('leaf', 'sub')), may hold values from -0.125 to 0.125
- mix: bfloat16 [512, 9, 2, 2, 128, 128], P(('leaf', 'sub')), may hold values from -0.25 to 0.25
- expand: bfloat16 [2, 128, 524288], P(None, None, ('leaf', 'sub')), may hold values from -0.375 to 0.375
Outputs:
- field: bfloat16 [2, 128, 524288], P(None, None, ('leaf', 'sub'))
The draws below stay inside these ranges and needn't reach their ends.
Inputs may be any that keep to these rules, and one draw needn't show every extreme that they name: `counts`: each box's count of live near-field boxes; box 0 has exactly 27. `neighbors`: slot 0 of each device's last box is 10, slot 0 of each device's first box is 1.
All inputs are finite; a program needn't handle non-finite values.
Results may differ from the reference program's by a relative error of at most 0.024.
Values may be sent and summed in bfloat16 or wider, within the bound.
No kernel may reach another device: no remote copies, remote signals or barrier semaphores. Data moves between devices by JAX's collectives and lax.ppermute only.
A program may use at most 64 MiB of HBM per device.

```python
import math
import jax
import jax.numpy as jnp
from jax import lax

NBOX = 8
BP = 128
R = 128
K = 27
HB = 2
NRHS = 128
LEVELS = 9
BOXES = 4096
PANELS = 524288
DEVICES = 512


def draw_counts(key, part):
    key = jax.random.fold_in(key, 11)
    level_key, count_key = jax.random.split(key)
    shift = jax.random.randint(level_key, (DEVICES,), 0, 4)
    ceiling = jnp.maximum(K // jnp.left_shift(jnp.ones_like(shift), shift), 1)
    ceiling_box = jnp.repeat(ceiling, NBOX)
    raw = jax.random.randint(count_key, (BOXES,), 0, 1 << 20)
    result = 1 + raw % ceiling_box
    result = result.at[0].set(K)
    return result.astype(jnp.int32)


def draw_neighbors(key, part):
    key = jax.random.fold_in(key, 12)
    lists = jax.random.randint(key, (BOXES, K), 0, NBOX + 2 * HB).astype(jnp.int32)
    local_box = jnp.arange(BOXES, dtype=jnp.int32) % NBOX
    first_slot = jnp.where(local_box == NBOX - 1, NBOX + HB, lists[:, 0])
    first_slot = jnp.where(local_box == 0, HB - 1, first_slot)
    lists = lists.at[:, 0].set(first_slot.astype(jnp.int32))
    return lists.astype(jnp.int32)


def touch_ends(values, stream_key, smallest, high):
    index_at = [jax.random.randint(jax.random.fold_in(stream_key, axis), (), 0, length) for axis, length in enumerate(values.shape)]
    main_axis = values.shape.index(max(values.shape))
    neighbour = index_at[:main_axis] + [(index_at[main_axis] + 1) % values.shape[main_axis]] + index_at[main_axis + 1:]
    return values.at[tuple(index_at)].set(smallest).at[tuple(neighbour)].set(high)


def level_of(stream_key, dims, cuts, least, high):
    def one(dim, parts):
        steps = jax.random.uniform(jax.random.fold_in(jax.random.fold_in(stream_key, 6), dim), (parts,), jnp.float32, least / len(cuts), high / len(cuts))
        return jnp.repeat(jnp.exp(steps), dims[dim] // parts).reshape((-1,) + (1,) * (len(dims) - dim - 1))

    loudness = one(*cuts[0])
    for cut in cuts[1:]:
        loudness = loudness * one(*cut)
    return loudness


def centred(rng, shape, scale, reach, cuts=(), held_as=jnp.bfloat16):
    loudness = level_of(rng, shape, cuts, -0.22, 0.18) if cuts else 1.0
    values = jax.random.normal(rng, shape, jnp.float32) * scale * loudness
    return jnp.minimum(jnp.maximum(values, -reach), reach).astype(held_as)


def setup_inputs(seed: int = 0) -> dict:
    key_of = jax.random.split(jax.random.key(seed), 10)
    return {
        "density": centred(key_of[0], (2, NRHS, PANELS), 1.0, 6.0, ((2, 512),)),
        "coords": centred(key_of[1], (3, PANELS), 0.5, 3.0, ((1, 512),)),
        "weights": jnp.clip(jnp.exp(math.log(0.33984375) - 2.3040229 * jax.random.uniform(key_of[2], (PANELS,), jnp.float32) ** level_of(key_of[2], (PANELS,), ((0, 512),), -0.2, 0.2)), 0.033935547, 0.33984375).astype(jnp.bfloat16),
        "counts": draw_counts(jax.random.fold_in(key_of[9], 71), 0),
        "neighbors": draw_neighbors(jax.random.fold_in(key_of[9], 71), 0),
        "skeleton": touch_ends(jax.random.randint(key_of[5], (DEVICES, R), 0, NBOX * BP), jax.random.fold_in(key_of[5], 1), 0, (NBOX * BP) - 1).astype(jnp.int32),
        "compress": centred(key_of[6], (2, R, PANELS), (2 * NBOX * BP) ** -0.5, 0.125, ((2, 512),)),
        "mix": centred(key_of[7], (DEVICES, LEVELS, 2, 2, R, R), (4 * R) ** -0.5, 0.25, ((0, 512),)),
        "expand": centred(key_of[8], (2, R, PANELS), (2 * R) ** -0.5, 0.375, ((2, 512),)),
    }


WAVE_NUMBER = 2.0 * math.pi
SOFTENING = 0.05
FOUR_PI = 4.0 * math.pi

def kernel_tiles(target, source, src_weight, live):
    spread = target[:, :, :, None] - source[:, :, None, :]
    radius = jnp.sqrt(lax.optimization_barrier(jnp.sum(spread * spread, axis=1)) + SOFTENING * SOFTENING)
    amplitude = live[:, None, None] * src_weight[:, None, :] / (FOUR_PI * radius)
    tile_real = (amplitude * jnp.cos(WAVE_NUMBER * radius)).astype(jnp.bfloat16)
    tile_imag = (amplitude * jnp.sin(WAVE_NUMBER * radius)).astype(jnp.bfloat16)
    return lax.optimization_barrier((tile_real, tile_imag))

def near_product(tile_real, tile_imag, sources):
    src = sources.astype(jnp.float32)
    real_part = jnp.einsum('kts,pcks->pct', tile_real.astype(jnp.float32), src)
    imag_part = jnp.einsum('kts,pcks->pct', tile_imag.astype(jnp.float32), src)
    return jnp.stack([real_part[0] - imag_part[1], real_part[1] + imag_part[0]])

def pair_product(left, right):
    left = left.astype(jnp.float32)
    right = right.astype(jnp.float32)
    real = jnp.einsum('cq,rq->cr', left[0], right[0]) - jnp.einsum('cq,rq->cr', left[1], right[1])
    imag = jnp.einsum('cq,rq->cr', left[0], right[1]) + jnp.einsum('cq,rq->cr', left[1], right[0])
    return jnp.stack([real, imag])

def expand_product(left, right):
    left = left.astype(jnp.float32)
    right = right.astype(jnp.float32)
    real = jnp.einsum('cr,rp->cp', left[0], right[0]) - jnp.einsum('cr,rp->cp', left[1], right[1])
    imag = jnp.einsum('cr,rp->cp', left[0], right[1]) + jnp.einsum('cr,rp->cp', left[1], right[0])
    return jnp.stack([real, imag])

def reference(density, coords, weights, counts, neighbors, skeleton, compress, mix, expand):
    panel_dev = NBOX * BP
    device_ids = jnp.arange(DEVICES, dtype=jnp.int32)
    slot_ids = jnp.arange(K, dtype=jnp.int32)
    inside = jnp.arange(BP, dtype=jnp.int32)

    def compress_one(device):
        start = (device * panel_dev).astype(jnp.int32)
        block = lax.dynamic_slice_in_dim(density, start, panel_dev, 2)
        basis = lax.dynamic_slice_in_dim(compress, start, panel_dev, 2)
        picked = jnp.take(block, skeleton[device], axis=2).astype(jnp.float32)
        return (picked + pair_product(block, basis)).astype(jnp.bfloat16)
    state = lax.map(compress_one, device_ids)
    for level in range(LEVELS):
        partner = state[device_ids ^ 1 << level]

        def mix_one(operands):
            own, other, matrices = operands
            total = pair_product(own, matrices[0]) + pair_product(other, matrices[1])
            return total.astype(jnp.bfloat16)
        state = lax.optimization_barrier(lax.map(mix_one, (state, partner, mix[:, level])))

    def near_box(box):
        device = box // NBOX
        source_box = (device * NBOX - HB + neighbors[box]).astype(jnp.int32)
        valid = (source_box >= 0) & (source_box < BOXES)
        live = ((slot_ids < counts[box]) & valid).astype(jnp.float32)
        safe_box = jnp.clip(source_box, 0, BOXES - 1)
        src_panel = safe_box[:, None] * BP + inside[None, :]
        target = coords[:, box * BP + inside].astype(jnp.float32)
        target = jnp.broadcast_to(target[None], (K, 3, BP))
        source = jnp.transpose(coords[:, src_panel].astype(jnp.float32), (1, 0, 2))
        src_weight = weights[src_panel].astype(jnp.float32)
        tile_real, tile_imag = kernel_tiles(target, source, src_weight, live)
        return near_product(tile_real, tile_imag, density[:, :, src_panel])

    def finish(operands):
        device, final = operands
        start = (device * panel_dev).astype(jnp.int32)
        basis = lax.dynamic_slice_in_dim(expand, start, panel_dev, 2)
        far = expand_product(final, basis)
        near = lax.map(near_box, device * NBOX + jnp.arange(NBOX, dtype=jnp.int32))
        near = jnp.transpose(near, (1, 2, 0, 3)).reshape(2, NRHS, panel_dev)
        return (far + near).astype(jnp.bfloat16)
    blocks = lax.map(finish, (device_ids, state))
    return jnp.transpose(blocks, (1, 2, 0, 3)).reshape(2, NRHS, PANELS)
```

```python
import functools
import math

import jax
import jax.numpy as jnp
from jax import lax
from jax.experimental import pallas as pl
from jax.experimental.pallas import tpu as pltpu
from jax.sharding import PartitionSpec as P

HB = 2
PACK = 16

SOFTENING = 0.05
FOUR_PI = 4.0 * math.pi

SIN_COEFFS = (4.442867902822206, -7.307443412968344, 3.5947879989545957, -0.7843738193353357)
COS_COEFFS = (1.4142134965639892, -6.978850988075765, 5.739461166775787, -1.8835629581956719, 0.3106981253821905)

NT = (((1,), (1,)), ((), ()))
NN = (((1,), (0,)), ((), ()))
TN = (((0,), (0,)), ((), ()))

VMEM_LIMIT = 16 * 1024 * 1024


def dot(left, right, dims):
    return lax.dot_general(left, right, dims, preferred_element_type=jnp.float32)


def horner(coeffs, x):
    total = coeffs[-1] * x + coeffs[-2]
    for c in reversed(coeffs[:-2]):
        total = total * x + c
    return total


def rows_of(values, rows, count):
    index = lax.broadcasted_iota(jnp.int32, (rows, count), 0)
    total = jnp.zeros((rows, count), jnp.float32)
    for i, value in enumerate(values):
        total = jnp.where(index == i, value, total)
    return total


def head_kernel(density, compress, skeleton, state):
    rank = skeleton.shape[1]
    panels = density.shape[1]
    columns = density.shape[0] // 2
    d = density[...]
    index = lax.broadcasted_iota(jnp.int32, (panels, rank), 0)
    onehot = (index == skeleton[...]).astype(jnp.float32).astype(jnp.bfloat16)
    picked = dot(d, onehot, NN)
    product = dot(d, compress[...], NT)
    real = product[:columns, :rank] - product[columns:, rank:] + picked[:columns]
    imag = product[:columns, rank:] + product[columns:, :rank] + picked[columns:]
    state[0] = real.astype(state.dtype)
    state[1] = imag.astype(state.dtype)


def pack_kernel(density, coords, weights, after, geometry, head, tail):
    del after
    panels = density.shape[1]
    width = head.shape[1]
    rows = density.shape[0]
    c = coords[...].astype(jnp.float32)
    w = weights[...].astype(jnp.float32)
    geo = rows_of([c[0:1], c[1:2], c[2:3], w], PACK, panels).astype(jnp.bfloat16)
    geometry[...] = geo
    head[0:rows, :] = density[:, 0:width]
    tail[0:rows, :] = density[:, panels - width : panels]
    head[rows : rows + PACK, :] = geo[:, 0:width]
    tail[rows : rows + PACK, :] = geo[:, panels - width : panels]


def near_kernel(first, counts, neighbors, density, geometry, left, right, after, out, tiles):
    del after
    rows, panels = density.shape
    columns = rows // 2
    halo = left.shape[1]
    wide = panels + 2 * halo
    box_count, slot_count = neighbors.shape
    size = panels // box_count
    wide_boxes = wide // size
    boxes = out.shape[2] // size

    geo = jnp.concatenate(
        [left[rows : rows + PACK, :], geometry[...], right[rows : rows + PACK, :]], axis=1
    ).astype(jnp.float32)
    x, y, z, w = geo[0:1], geo[1:2], geo[2:3], geo[3:4]
    square = x * x + y * y + z * z

    def split(value):
        one = value.astype(jnp.bfloat16).astype(jnp.float32)
        two = (value - one).astype(jnp.bfloat16).astype(jnp.float32)
        return [one, two, value - one - two]

    ones = jnp.ones_like(x)
    source = rows_of(
        [x, y, z] + split(square + SOFTENING * SOFTENING) + [ones] * 3, PACK, wide
    ).astype(jnp.bfloat16)

    slots = neighbors[...]
    live_count = jnp.zeros((box_count, 1), jnp.int32)
    box_id = lax.broadcasted_iota(jnp.int32, (box_count, 1), 0)
    for b in range(box_count):
        live_count = jnp.where(box_id == b, counts[b], live_count)
    slot_id = lax.broadcasted_iota(jnp.int32, (box_count, slot_count), 1)
    slots = jnp.where(slot_id < live_count, slots, -1)
    times = [
        jnp.sum(jnp.where(slots == g, 1.0, 0.0), axis=1, keepdims=True) for g in range(wide_boxes)
    ]

    for i in range(boxes):
        b = first + i
        start = halo + b * size
        at = slice(start, start + size)
        target = rows_of(
            [-2.0 * x[:, at], -2.0 * y[:, at], -2.0 * z[:, at]] + [ones[:, at]] * 3 + split(square[:, at]),
            PACK,
            size,
        ).astype(jnp.bfloat16)
        for g in range(0, wide_boxes, 2):
            span = slice(g * size, (g + 2) * size)
            r2 = dot(target, source[:, span], TN)
            inverse = lax.rsqrt(r2)
            radius = r2 * inverse
            f = radius - jnp.round(radius)
            q = f * f
            u = f * horner(SIN_COEFFS, q)
            v = horner(COS_COEFFS, q)
            factor = w[:, span] * (1.0 / FOUR_PI)
            many = jnp.concatenate(
                [jnp.broadcast_to(times[g + j][b : b + 1], (1, size)) for j in range(2)], axis=1
            )
            a = inverse * (factor * many)
            au = a * u
            tiles[i, 0:size, span] = (a - au * u).astype(jnp.bfloat16)
            tiles[i, size : 2 * size, span] = (au * v).astype(jnp.bfloat16)
        total = dot(density[...], tiles[i, :, halo : halo + panels], NT)
        total += dot(left[0:rows, :], tiles[i, :, 0:halo], NT)
        total += dot(right[0:rows, :], tiles[i, :, halo + panels : wide], NT)
        place = slice(i * size, (i + 1) * size)
        out[0, :, place] = total[:columns, :size] - total[columns:, size:]
        out[1, :, place] = total[:columns, size:] + total[columns:, :size]


def tail_kernel(state, expand, near, out):
    columns = state.shape[1]
    rank = state.shape[2]
    s = state[...].reshape(2 * columns, rank)
    first = dot(s, expand[0], NN)
    second = dot(s, expand[1], NN)
    real = first[:columns] - second[columns:]
    imag = second[:columns] + first[columns:]
    out[0] = (real + near[0]).astype(out.dtype)
    out[1] = (imag + near[1]).astype(out.dtype)


def params():
    return pltpu.CompilerParams(vmem_limit_bytes=VMEM_LIMIT)


def in_vmem():
    return pl.BlockSpec(memory_space=pltpu.VMEM)


def anywhere():
    return pl.BlockSpec(memory_space=pl.ANY)


def exchange(value, axis, stride):
    mask = 2**stride
    pairs = [(source, source ^ mask) for source in range(lax.axis_size(axis))]
    return lax.ppermute(value, axis, pairs)


def shift(value, step):
    axes = ("leaf", "sub")
    count = lax.axis_size(axes)
    if step > 0:
        pairs = [(i, i + 1) for i in range(count - 1)]
    else:
        pairs = [(i + 1, i) for i in range(count - 1)]
    return lax.ppermute(value, axes, pairs)


def pair_product(left, right):
    columns = left.shape[1]
    rank_rows = right.shape[1]
    product = dot(left.reshape(2 * columns, -1), right.reshape(2 * rank_rows, -1), NT)
    real = product[:columns, :rank_rows] - product[columns:, rank_rows:]
    imag = product[:columns, rank_rows:] + product[columns:, :rank_rows]
    return jnp.stack([real, imag])


def combine(own, other, matrices):
    return (pair_product(own, matrices[0]) + pair_product(other, matrices[1])).astype(jnp.bfloat16)


def per_device(density, coords, weights, counts, neighbors, skeleton, compress, mix, expand):
    columns, panels = density.shape[1:]
    rank = compress.shape[1]
    box_count = counts.shape[0]
    size = panels // box_count
    halo = HB * size
    rows = 2 * columns
    flat = density.reshape(rows, panels)
    basis = compress.reshape(2 * rank, panels)

    state = pl.pallas_call(
        head_kernel,
        out_shape=jax.ShapeDtypeStruct((2, columns, rank), jnp.bfloat16),
        in_specs=[in_vmem()] * 3,
        out_specs=in_vmem(),
        compiler_params=params(),
        cost_estimate=pl.CostEstimate(flops=2 * rows * panels * 3 * rank, bytes_accessed=2**20, transcendentals=0),
        name="compress_density",
    )(flat, basis, skeleton)

    strip = jax.ShapeDtypeStruct((rows + PACK, halo), jnp.bfloat16)
    geometry, head, tail = pl.pallas_call(
        pack_kernel,
        out_shape=(jax.ShapeDtypeStruct((PACK, panels), jnp.bfloat16), strip, strip),
        in_specs=[in_vmem()] * 3 + [anywhere()],
        out_specs=(in_vmem(),) * 3,
        compiler_params=params(),
        cost_estimate=pl.CostEstimate(flops=2**20, bytes_accessed=2**20, transcendentals=0),
        name="pack_halo",
    )(flat, coords, weights[None, :], state)
    left = shift(tail, 1)
    right = shift(head, -1)

    sub_levels = lax.axis_size("sub").bit_length() - 1
    leaf_levels = lax.axis_size("leaf").bit_length() - 1
    steps = [("sub", i) for i in range(sub_levels)] + [("leaf", i) for i in range(leaf_levels)]
    per_call = 2
    calls = box_count // per_call
    begin = 3
    near = []

    def near_boxes(after):
        call = pl.pallas_call(
            functools.partial(near_kernel, len(near) * per_call),
            out_shape=jax.ShapeDtypeStruct((2, columns, per_call * size), jnp.float32),
            in_specs=[pl.BlockSpec(memory_space=pltpu.SMEM)] + [in_vmem()] * 5 + [anywhere()],
            out_specs=in_vmem(),
            scratch_shapes=[pltpu.VMEM((per_call, 2 * size, panels + 2 * halo), jnp.bfloat16)],
            compiler_params=params(),
            cost_estimate=pl.CostEstimate(
                flops=2 * per_call * rows * (panels + 2 * halo) * 2 * size,
                bytes_accessed=2**21,
                transcendentals=per_call * size * (panels + 2 * halo),
            ),
            name="near_boxes",
        )
        near.append(call(counts, neighbors, flat, geometry, left, right, after))

    for level, (axis, stride) in enumerate(steps):
        other = exchange(state, axis, stride)
        if level >= begin and len(near) < calls:
            near_boxes(state)
        state = combine(state, other, mix[0, level])
    while len(near) < calls:
        near_boxes(state)

    near = jnp.concatenate(near, axis=2)
    block = 2 * size
    return pl.pallas_call(
        tail_kernel,
        grid=(panels // block,),
        out_shape=jax.ShapeDtypeStruct((2, columns, panels), jnp.bfloat16),
        in_specs=[
            pl.BlockSpec((2, columns, rank), lambda i: (0, 0, 0)),
            pl.BlockSpec((2, rank, block), lambda i: (0, 0, i)),
            pl.BlockSpec((2, columns, block), lambda i: (0, 0, i)),
        ],
        out_specs=pl.BlockSpec((2, columns, block), lambda i: (0, 0, i)),
        compiler_params=params(),
        cost_estimate=pl.CostEstimate(flops=4 * rows * rank * panels, bytes_accessed=2**21, transcendentals=0),
        name="expand_state",
    )(state, expand, near)


def solution(mesh):
    return jax.shard_map(
        per_device,
        mesh=mesh,
        in_specs=(
            P(None, None, ("leaf", "sub")),
            P(None, ("leaf", "sub")),
            P(("leaf", "sub")),
            P(("leaf", "sub")),
            P(("leaf", "sub"), None),
            P(("leaf", "sub"), None),
            P(None, None, ("leaf", "sub")),
            P(("leaf", "sub"), None, None, None, None, None),
            P(None, None, ("leaf", "sub")),
        ),
        out_specs=P(None, None, ("leaf", "sub")),
        check_vma=False,
    )
```

```python
import functools
import math

import jax
import jax.numpy as jnp
from jax import lax
from jax.experimental import pallas as pl
from jax.experimental.pallas import tpu as pltpu
from jax.sharding import PartitionSpec as P

HB = 2
PACK = 16

SOFTENING = 0.05
FOUR_PI = 4.0 * math.pi

SIN_COEFFS = (4.442867902822206, -7.307443412968344, 3.5947879989545957, -0.7843738193353357)
COS_COEFFS = (1.4142134965639892, -6.978850988075765, 5.739461166775787, -1.8835629581956719, 0.3106981253821905)

NT = (((1,), (1,)), ((), ()))
NN = (((1,), (0,)), ((), ()))
TN = (((0,), (0,)), ((), ()))

VMEM_LIMIT = 16 * 1024 * 1024
WHOLE_VMEM = 63 * 1024 * 1024


def dot(left, right, dims):
    return lax.dot_general(left, right, dims, preferred_element_type=jnp.float32)


def horner(coeffs, x):
    total = coeffs[-1] * x + coeffs[-2]
    for c in reversed(coeffs[:-2]):
        total = total * x + c
    return total


def rows_of(values, rows, count):
    index = lax.broadcasted_iota(jnp.int32, (rows, count), 0)
    total = jnp.zeros((rows, count), jnp.float32)
    for i, value in enumerate(values):
        total = jnp.where(index == i, value, total)
    return total


def head_kernel(skeleton_hbm, density_hbm, compress_hbm, state, skeleton, density, compress, sems):
    copies = [
        pltpu.make_async_copy(skeleton_hbm, skeleton, sems.at[0]),
        pltpu.make_async_copy(density_hbm, density, sems.at[1]),
        pltpu.make_async_copy(compress_hbm, compress, sems.at[2]),
    ]
    for copy in copies:
        copy.start()
    rank = skeleton.shape[1]
    panels = density.shape[1]
    columns = density.shape[0] // 2
    index = lax.broadcasted_iota(jnp.int32, (panels, rank), 0)
    copies[0].wait()
    onehot = (index == skeleton[...]).astype(jnp.float32).astype(jnp.bfloat16)
    copies[1].wait()
    d = density[...]
    picked = dot(d, onehot, NN)
    copies[2].wait()
    product = dot(d, compress[...], NT)
    real = product[:columns, :rank] - product[columns:, rank:] + picked[:columns]
    imag = product[:columns, rank:] + product[columns:, :rank] + picked[columns:]
    state[0] = real.astype(state.dtype)
    state[1] = imag.astype(state.dtype)


def geometry_rows(coords, weights, count):
    c = coords.astype(jnp.float32)
    w = weights.astype(jnp.float32)
    return rows_of([c[0:1], c[1:2], c[2:3], w], PACK, count).astype(jnp.bfloat16)


def tail_strip_kernel(density, coords, weights, after, geometry, strip):
    del after
    rows, panels = density.shape
    width = strip.shape[1]
    geo = geometry_rows(coords[...], weights[...], panels)
    geometry[...] = geo
    strip[0:rows, :] = density[:, panels - width : panels]
    strip[rows : rows + PACK, :] = geo[:, panels - width : panels]


def head_strip_kernel(density, geometry, after, strip):
    del after
    rows = density.shape[0]
    width = strip.shape[1]
    strip[0:rows, :] = density[:, 0:width]
    strip[rows : rows + PACK, :] = geometry[:, 0:width]


def near_kernel(first, counts, neighbors, density, geometry, left, right, after, out, tiles):
    del after
    rows, panels = density.shape
    columns = rows // 2
    halo = left.shape[1]
    wide = panels + 2 * halo
    box_count, slot_count = neighbors.shape
    size = panels // box_count
    wide_boxes = wide // size
    boxes = out.shape[2] // size

    geo = jnp.concatenate(
        [left[rows : rows + PACK, :], geometry[...], right[rows : rows + PACK, :]], axis=1
    ).astype(jnp.float32)
    x, y, z, w = geo[0:1], geo[1:2], geo[2:3], geo[3:4]
    square = x * x + y * y + z * z

    def split(value):
        one = value.astype(jnp.bfloat16).astype(jnp.float32)
        two = (value - one).astype(jnp.bfloat16).astype(jnp.float32)
        return [one, two, value - one - two]

    ones = jnp.ones_like(x)
    source = rows_of(
        [x, y, z] + split(square + SOFTENING * SOFTENING) + [ones] * 3, PACK, wide
    ).astype(jnp.bfloat16)

    slots = neighbors[...]
    live_count = jnp.zeros((box_count, 1), jnp.int32)
    box_id = lax.broadcasted_iota(jnp.int32, (box_count, 1), 0)
    for b in range(box_count):
        live_count = jnp.where(box_id == b, counts[b], live_count)
    slot_id = lax.broadcasted_iota(jnp.int32, (box_count, slot_count), 1)
    slots = jnp.where(slot_id < live_count, slots, -1)
    times = [
        jnp.sum(jnp.where(slots == g, 1.0, 0.0), axis=1, keepdims=True) for g in range(wide_boxes)
    ]

    for i in range(boxes):
        b = first + i
        start = halo + b * size
        at = slice(start, start + size)
        target = rows_of(
            [-2.0 * x[:, at], -2.0 * y[:, at], -2.0 * z[:, at]] + [ones[:, at]] * 3 + split(square[:, at]),
            PACK,
            size,
        ).astype(jnp.bfloat16)
        for g in range(0, wide_boxes, 2):
            span = slice(g * size, (g + 2) * size)
            r2 = dot(target, source[:, span], TN)
            inverse = lax.rsqrt(r2)
            radius = r2 * inverse
            f = radius - jnp.round(radius)
            q = f * f
            u = f * horner(SIN_COEFFS, q)
            v = horner(COS_COEFFS, q)
            factor = w[:, span] * (1.0 / FOUR_PI)
            many = jnp.concatenate(
                [jnp.broadcast_to(times[g + j][b : b + 1], (1, size)) for j in range(2)], axis=1
            )
            a = inverse * (factor * many)
            au = a * u
            tiles[i, 0:size, span] = (a - au * u).astype(jnp.bfloat16)
            tiles[i, size : 2 * size, span] = (au * v).astype(jnp.bfloat16)
        total = dot(density[...], tiles[i, :, halo : halo + panels], NT)
        total += dot(left[0:rows, :], tiles[i, :, 0:halo], NT)
        total += dot(right[0:rows, :], tiles[i, :, halo + panels : wide], NT)
        place = slice(i * size, (i + 1) * size)
        out[0, :, place] = total[:columns, :size] - total[columns:, size:]
        out[1, :, place] = total[:columns, size:] + total[columns:, :size]


def tail_kernel(state, expand, near, out, block, sems):
    columns, rank = state.shape[1:]
    panels = expand.shape[2]
    step = panels // sems.shape[0]
    s = state[...].reshape(2 * columns, rank)
    copies = []
    for i in range(sems.shape[0]):
        at = slice(i * step, (i + 1) * step)
        first = dot(s, expand[0, :, at], NN)
        second = dot(s, expand[1, :, at], NN)
        real = first[:columns] - second[columns:]
        imag = second[:columns] + first[columns:]
        block[0, :, at] = (real + near[0, :, at]).astype(block.dtype)
        block[1, :, at] = (imag + near[1, :, at]).astype(block.dtype)
        copies.append(pltpu.make_async_copy(block.at[:, :, at], out.at[:, :, at], sems.at[i]))
        copies[-1].start()
    for copy in copies:
        copy.wait()


def params(limit=VMEM_LIMIT):
    return pltpu.CompilerParams(vmem_limit_bytes=limit)


def in_vmem():
    return pl.BlockSpec(memory_space=pltpu.VMEM)


def anywhere():
    return pl.BlockSpec(memory_space=pl.ANY)


def exchange(value, axis, stride):
    mask = 2**stride
    pairs = [(source, source ^ mask) for source in range(lax.axis_size(axis))]
    return lax.ppermute(value, axis, pairs)


def shift(value, step):
    axes = ("leaf", "sub")
    count = lax.axis_size(axes)
    if step > 0:
        pairs = [(i, i + 1) for i in range(count - 1)]
    else:
        pairs = [(i + 1, i) for i in range(count - 1)]
    return lax.ppermute(value, axes, pairs)


def pair_product(left, right):
    columns = left.shape[1]
    rank_rows = right.shape[1]
    product = dot(left.reshape(2 * columns, -1), right.reshape(2 * rank_rows, -1), NT)
    real = product[:columns, :rank_rows] - product[columns:, rank_rows:]
    imag = product[:columns, rank_rows:] + product[columns:, :rank_rows]
    return jnp.stack([real, imag])


def combine(own, other, matrices):
    return (pair_product(own, matrices[0]) + pair_product(other, matrices[1])).astype(jnp.bfloat16)


def per_device(density, coords, weights, counts, neighbors, skeleton, compress, mix, expand):
    columns, panels = density.shape[1:]
    rank = compress.shape[1]
    box_count = counts.shape[0]
    size = panels // box_count
    halo = HB * size
    rows = 2 * columns
    flat = density.reshape(rows, panels)
    basis = compress.reshape(2 * rank, panels)

    state = pl.pallas_call(
        head_kernel,
        out_shape=jax.ShapeDtypeStruct((2, columns, rank), jnp.bfloat16),
        in_specs=[pl.BlockSpec(memory_space=pltpu.HBM)] * 3,
        out_specs=in_vmem(),
        scratch_shapes=[
            pltpu.VMEM(skeleton.shape, skeleton.dtype),
            pltpu.VMEM(flat.shape, flat.dtype),
            pltpu.VMEM(basis.shape, basis.dtype),
            pltpu.SemaphoreType.DMA((3,)),
        ],
        compiler_params=params(WHOLE_VMEM),
        cost_estimate=pl.CostEstimate(flops=2 * rows * panels * 3 * rank, bytes_accessed=2**20, transcendentals=0),
        name="compress_density",
    )(skeleton, flat, basis)

    strip = jax.ShapeDtypeStruct((rows + PACK, halo), jnp.bfloat16)
    cheap = pl.CostEstimate(flops=2**20, bytes_accessed=2**18, transcendentals=0)

    def tail_strip(after):
        return pl.pallas_call(
            tail_strip_kernel,
            out_shape=(jax.ShapeDtypeStruct((PACK, panels), jnp.bfloat16), strip),
            in_specs=[in_vmem()] * 3 + [anywhere()],
            out_specs=(in_vmem(),) * 2,
            compiler_params=params(),
            cost_estimate=cheap,
            name="tail_strip",
        )(flat, coords, weights[None, :], after)

    def head_strip(after):
        return pl.pallas_call(
            head_strip_kernel,
            out_shape=strip,
            in_specs=[in_vmem()] * 2 + [anywhere()],
            out_specs=in_vmem(),
            compiler_params=params(),
            cost_estimate=cheap,
            name="head_strip",
        )(flat, geometry, after)

    sub_levels = lax.axis_size("sub").bit_length() - 1
    leaf_levels = lax.axis_size("leaf").bit_length() - 1
    steps = [("sub", i) for i in range(sub_levels)] + [("leaf", i) for i in range(leaf_levels)]
    per_call = 2
    calls = box_count // per_call
    near = []

    def near_boxes(after):
        call = pl.pallas_call(
            functools.partial(near_kernel, len(near) * per_call),
            out_shape=jax.ShapeDtypeStruct((2, columns, per_call * size), jnp.float32),
            in_specs=[pl.BlockSpec(memory_space=pltpu.SMEM)] + [in_vmem()] * 5 + [anywhere()],
            out_specs=in_vmem(),
            scratch_shapes=[pltpu.VMEM((per_call, 2 * size, panels + 2 * halo), jnp.bfloat16)],
            compiler_params=params(),
            cost_estimate=pl.CostEstimate(
                flops=2 * per_call * rows * (panels + 2 * halo) * 2 * size,
                bytes_accessed=2**21,
                transcendentals=per_call * size * (panels + 2 * halo),
            ),
            name="near_boxes",
        )
        near.append(call(counts, neighbors, flat, geometry, left, right, after))

    for level, (axis, stride) in enumerate(steps):
        other = exchange(state, axis, stride)
        if level == 1:
            geometry, strip_out = tail_strip(state)
            left = shift(strip_out, 1)
        if level == 2:
            right = shift(head_strip(state), -1)
        if level in (4, 5):
            near_boxes(state)
            near_boxes(state)
        state = combine(state, other, mix[0, level])
    while len(near) < calls:
        near_boxes(state)

    near = jnp.concatenate(near, axis=2)
    return pl.pallas_call(
        tail_kernel,
        out_shape=jax.ShapeDtypeStruct((2, columns, panels), jnp.bfloat16),
        in_specs=[in_vmem()] * 3,
        out_specs=anywhere(),
        scratch_shapes=[pltpu.VMEM((2, columns, panels), jnp.bfloat16), pltpu.SemaphoreType.DMA((4,))],
        compiler_params=params(),
        cost_estimate=pl.CostEstimate(flops=4 * rows * rank * panels, bytes_accessed=2**21, transcendentals=0),
        name="expand_state",
    )(state, expand, near)


def solution(mesh):
    return jax.shard_map(
        per_device,
        mesh=mesh,
        in_specs=(
            P(None, None, ("leaf", "sub")),
            P(None, ("leaf", "sub")),
            P(("leaf", "sub")),
            P(("leaf", "sub")),
            P(("leaf", "sub"), None),
            P(("leaf", "sub"), None),
            P(None, None, ("leaf", "sub")),
            P(("leaf", "sub"), None, None, None, None, None),
            P(None, None, ("leaf", "sub")),
        ),
        out_specs=P(None, None, ("leaf", "sub")),
        check_vma=False,
    )
```

```python
import functools
import math

import jax
import jax.numpy as jnp
from jax import lax
from jax.experimental import pallas as pl
from jax.experimental.pallas import tpu as pltpu
from jax.sharding import PartitionSpec as P

HB = 2
PACK = 16

SOFTENING = 0.05
FOUR_PI = 4.0 * math.pi

SIN_COEFFS = (4.442867902822206, -7.307443412968344, 3.5947879989545957, -0.7843738193353357)
COS_COEFFS = (1.4142134965639892, -6.978850988075765, 5.739461166775787, -1.8835629581956719, 0.3106981253821905)

NT = (((1,), (1,)), ((), ()))
NN = (((1,), (0,)), ((), ()))
TN = (((0,), (0,)), ((), ()))

NEAR_PLAN = {4: 1, 5: 2, 6: 1, 7: 2}
SECOND_HALO = 3

VMEM_LIMIT = 16 * 1024 * 1024
WHOLE_VMEM = 63 * 1024 * 1024


def dot(left, right, dims):
    return lax.dot_general(left, right, dims, preferred_element_type=jnp.float32)


def horner(coeffs, x):
    total = coeffs[-1] * x + coeffs[-2]
    for c in reversed(coeffs[:-2]):
        total = total * x + c
    return total


def rows_of(values, rows, count):
    index = lax.broadcasted_iota(jnp.int32, (rows, count), 0)
    total = jnp.zeros((rows, count), jnp.float32)
    for i, value in enumerate(values):
        total = jnp.where(index == i, value, total)
    return total


def head_kernel(skeleton_hbm, density_hbm, compress_hbm, state, skeleton, density, compress, sems):
    copies = [
        pltpu.make_async_copy(skeleton_hbm, skeleton, sems.at[0]),
        pltpu.make_async_copy(density_hbm, density, sems.at[1]),
        pltpu.make_async_copy(compress_hbm, compress, sems.at[2]),
    ]
    for copy in copies:
        copy.start()
    rank = skeleton.shape[1]
    panels = density.shape[1]
    columns = density.shape[0] // 2
    index = lax.broadcasted_iota(jnp.int32, (panels, rank), 0)
    copies[0].wait()
    onehot = (index == skeleton[...]).astype(jnp.float32).astype(jnp.bfloat16)
    copies[1].wait()
    d = density[...]
    picked = dot(d, onehot, NN)
    copies[2].wait()
    product = dot(d, compress[...], NT)
    real = product[:columns, :rank] - product[columns:, rank:] + picked[:columns]
    imag = product[:columns, rank:] + product[columns:, :rank] + picked[columns:]
    state[0] = real.astype(state.dtype)
    state[1] = imag.astype(state.dtype)


def geometry_rows(coords, weights, count):
    c = coords.astype(jnp.float32)
    w = weights.astype(jnp.float32)
    return rows_of([c[0:1], c[1:2], c[2:3], w], PACK, count).astype(jnp.bfloat16)


def tail_strip_kernel(density, coords, weights, after, geometry, strip):
    del after
    rows, panels = density.shape
    width = strip.shape[1]
    geo = geometry_rows(coords[...], weights[...], panels)
    geometry[...] = geo
    strip[0:rows, :] = density[:, panels - width : panels]
    strip[rows : rows + PACK, :] = geo[:, panels - width : panels]


def head_strip_kernel(density, geometry, after, strip):
    del after
    rows = density.shape[0]
    width = strip.shape[1]
    strip[0:rows, :] = density[:, 0:width]
    strip[rows : rows + PACK, :] = geometry[:, 0:width]


def prepare_kernel(counts, neighbors, geometry, left, right, source, target, factor):
    rows = left.shape[0] - PACK
    panels = geometry.shape[1]
    halo = left.shape[1]
    wide = panels + 2 * halo
    box_count, slot_count = neighbors.shape
    size = panels // box_count

    geo = jnp.concatenate(
        [left[rows : rows + PACK, :], geometry[...], right[rows : rows + PACK, :]], axis=1
    ).astype(jnp.float32)
    x, y, z, w = geo[0:1], geo[1:2], geo[2:3], geo[3:4]
    square = x * x + y * y + z * z

    def split(value):
        one = value.astype(jnp.bfloat16).astype(jnp.float32)
        two = (value - one).astype(jnp.bfloat16).astype(jnp.float32)
        return [one, two, value - one - two]

    ones = jnp.ones_like(x)
    source[...] = rows_of(
        [x, y, z] + split(square + SOFTENING * SOFTENING) + [ones] * 3, PACK, wide
    ).astype(jnp.bfloat16)
    at = slice(halo, halo + panels)
    target[...] = rows_of(
        [-2.0 * x[:, at], -2.0 * y[:, at], -2.0 * z[:, at]] + [ones[:, at]] * 3 + split(square[:, at]),
        PACK,
        panels,
    ).astype(jnp.bfloat16)

    slots = neighbors[...]
    live_count = jnp.zeros((box_count, 1), jnp.int32)
    box_id = lax.broadcasted_iota(jnp.int32, (box_count, 1), 0)
    for b in range(box_count):
        live_count = jnp.where(box_id == b, counts[b], live_count)
    slot_id = lax.broadcasted_iota(jnp.int32, (box_count, slot_count), 1)
    slots = jnp.where(slot_id < live_count, slots, -1)
    for g in range(wide // size):
        times = jnp.sum(jnp.where(slots == g, 1.0 / FOUR_PI, 0.0), axis=1, keepdims=True)
        span = slice(g * size, (g + 1) * size)
        factor[:, span] = times * w[:, span]


def near_kernel(first, density, left, right, source, target, factor, after, out, tiles):
    del after
    rows, panels = density.shape
    columns = rows // 2
    halo = left.shape[1]
    wide = panels + 2 * halo
    size = panels // factor.shape[0]
    chunk = 2 * size

    for i in range(out.shape[2] // size):
        b = first + i
        mine = target[:, b * size : (b + 1) * size]
        for begin in range(0, wide, chunk):
            span = slice(begin, begin + chunk)
            r2 = dot(mine, source[:, span], TN)
            inverse = lax.rsqrt(r2)
            radius = r2 * inverse
            f = radius - jnp.round(radius)
            q = f * f
            u = f * horner(SIN_COEFFS, q)
            v = horner(COS_COEFFS, q)
            a = inverse * factor[b : b + 1, span]
            au = a * u
            tiles[i, 0:size, span] = (a - au * u).astype(jnp.bfloat16)
            tiles[i, size : 2 * size, span] = (au * v).astype(jnp.bfloat16)
        total = dot(density[...], tiles[i, :, halo : halo + panels], NT)
        total += dot(left[0:rows, :], tiles[i, :, 0:halo], NT)
        total += dot(right[0:rows, :], tiles[i, :, halo + panels : wide], NT)
        place = slice(i * size, (i + 1) * size)
        out[0, :, place] = total[:columns, :size] - total[columns:, size:]
        out[1, :, place] = total[:columns, size:] + total[columns:, :size]


def flatten(pair):
    return pair.reshape(2 * pair.shape[1], pair.shape[2])


def add_level(level, own, other, mix):
    columns, rank = own.shape[1:]
    product = dot(flatten(other[...]), flatten(mix[level, 1]), NT)
    real = own[0] + product[:columns, :rank] - product[columns:, rank:]
    imag = own[1] + product[:columns, rank:] + product[columns:, :rank]
    return real.astype(jnp.bfloat16), imag.astype(jnp.bfloat16)


def level_kernel(level, own, other, mix, *rest):
    out = rest[-1]
    out[0], out[1] = add_level(level, own, other, mix)


def tail_kernel(level, own, other, mix, expand, *rest):
    near, (out, block, sems) = rest[:-3], rest[-3:]
    columns = own.shape[1]
    s = jnp.concatenate(add_level(level, own, other, mix), axis=0)
    copies = []
    start = 0
    for i, piece in enumerate(near):
        at = slice(start, start + piece.shape[2])
        start += piece.shape[2]
        first = dot(s, expand[0, :, at], NN)
        second = dot(s, expand[1, :, at], NN)
        real = first[:columns] - second[columns:]
        imag = second[:columns] + first[columns:]
        block[0, :, at] = (real + piece[0]).astype(block.dtype)
        block[1, :, at] = (imag + piece[1]).astype(block.dtype)
        copies.append(pltpu.make_async_copy(block.at[:, :, at], out.at[:, :, at], sems.at[i]))
        copies[-1].start()
    for copy in copies:
        copy.wait()


def params(limit=VMEM_LIMIT):
    return pltpu.CompilerParams(vmem_limit_bytes=limit)


def in_vmem():
    return pl.BlockSpec(memory_space=pltpu.VMEM)


def anywhere():
    return pl.BlockSpec(memory_space=pl.ANY)


def exchange(value, axis, stride):
    mask = 2**stride
    pairs = [(source, source ^ mask) for source in range(lax.axis_size(axis))]
    return lax.ppermute(value, axis, pairs)


def shift(value, step):
    axes = ("leaf", "sub")
    count = lax.axis_size(axes)
    if step > 0:
        pairs = [(i, i + 1) for i in range(count - 1)]
    else:
        pairs = [(i + 1, i) for i in range(count - 1)]
    return lax.ppermute(value, axes, pairs)


def pair_product(left, right):
    columns = left.shape[1]
    rank_rows = right.shape[1]
    product = dot(left.reshape(2 * columns, -1), right.reshape(2 * rank_rows, -1), NT)
    real = product[:columns, :rank_rows] - product[columns:, rank_rows:]
    imag = product[:columns, rank_rows:] + product[columns:, :rank_rows]
    return jnp.stack([real, imag])


def per_device(density, coords, weights, counts, neighbors, skeleton, compress, mix, expand):
    columns, panels = density.shape[1:]
    rank = compress.shape[1]
    box_count = counts.shape[0]
    size = panels // box_count
    halo = HB * size
    rows = 2 * columns
    flat = density.reshape(rows, panels)
    basis = compress.reshape(2 * rank, panels)

    state = pl.pallas_call(
        head_kernel,
        out_shape=jax.ShapeDtypeStruct((2, columns, rank), jnp.bfloat16),
        in_specs=[pl.BlockSpec(memory_space=pltpu.HBM)] * 3,
        out_specs=in_vmem(),
        scratch_shapes=[
            pltpu.VMEM(skeleton.shape, skeleton.dtype),
            pltpu.VMEM(flat.shape, flat.dtype),
            pltpu.VMEM(basis.shape, basis.dtype),
            pltpu.SemaphoreType.DMA((3,)),
        ],
        compiler_params=params(WHOLE_VMEM),
        cost_estimate=pl.CostEstimate(flops=2 * rows * panels * 3 * rank, bytes_accessed=2**20, transcendentals=0),
        name="compress_density",
    )(skeleton, flat, basis)

    strip = jax.ShapeDtypeStruct((rows + PACK, halo), jnp.bfloat16)
    cheap = pl.CostEstimate(flops=2**20, bytes_accessed=2**18, transcendentals=0)

    def tail_strip(after):
        return pl.pallas_call(
            tail_strip_kernel,
            out_shape=(jax.ShapeDtypeStruct((PACK, panels), jnp.bfloat16), strip),
            in_specs=[in_vmem()] * 3 + [anywhere()],
            out_specs=(in_vmem(),) * 2,
            compiler_params=params(),
            cost_estimate=cheap,
            name="tail_strip",
        )(flat, coords, weights[None, :], after)

    def head_strip(after):
        return pl.pallas_call(
            head_strip_kernel,
            out_shape=strip,
            in_specs=[in_vmem()] * 2 + [anywhere()],
            out_specs=in_vmem(),
            compiler_params=params(),
            cost_estimate=cheap,
            name="head_strip",
        )(flat, geometry, after)

    sub_levels = lax.axis_size("sub").bit_length() - 1
    leaf_levels = lax.axis_size("leaf").bit_length() - 1
    steps = [("sub", i) for i in range(sub_levels)] + [("leaf", i) for i in range(leaf_levels)]
    mixes = mix[0]
    wide = panels + 2 * halo

    def kernel(body, out_shape, operands, after=(), scratch=(), cost=cheap, name=None):
        one = not isinstance(out_shape, tuple)
        return pl.pallas_call(
            body,
            out_shape=out_shape,
            in_specs=[in_vmem()] * len(operands) + [anywhere()] * len(after),
            out_specs=in_vmem() if one else (in_vmem(),) * len(out_shape),
            scratch_shapes=list(scratch),
            compiler_params=params(),
            cost_estimate=cost,
            name=name,
        )(*operands, *after)

    def prepare():
        return pl.pallas_call(
            prepare_kernel,
            out_shape=(
                jax.ShapeDtypeStruct((PACK, wide), jnp.bfloat16),
                jax.ShapeDtypeStruct((PACK, panels), jnp.bfloat16),
                jax.ShapeDtypeStruct((box_count, wide), jnp.float32),
            ),
            in_specs=[pl.BlockSpec(memory_space=pltpu.SMEM)] + [in_vmem()] * 4,
            out_specs=(in_vmem(),) * 3,
            compiler_params=params(),
            cost_estimate=cheap,
            name="prepare_near",
        )(counts, neighbors, geometry, left, right)

    def near_boxes(first, boxes, after):
        return kernel(
            functools.partial(near_kernel, first),
            jax.ShapeDtypeStruct((2, columns, boxes * size), jnp.float32),
            [flat, left, right, source, target, factor],
            [after],
            [pltpu.VMEM((boxes, 2 * size, wide), jnp.bfloat16)],
            pl.CostEstimate(
                flops=2 * boxes * rows * wide * 2 * size, bytes_accessed=2**21, transcendentals=boxes * size * wide
            ),
            "near_boxes",
        )

    near = []
    done = 0
    last = len(steps) - 1
    for level, (axis, stride) in enumerate(steps):
        other = exchange(state, axis, stride)
        own = pair_product(state, mixes[level, 0])
        ties = []
        if level == 1:
            geometry, strip_out = tail_strip(state)
            left = shift(strip_out, 1)
        if level == min(SECOND_HALO, last):
            right = shift(head_strip(state), -1)
        boxes = box_count - done if level == last else NEAR_PLAN.get(level, 0)
        if boxes:
            if not near:
                source, target, factor = prepare()
            near.append(near_boxes(done, boxes, state))
            done += boxes
            ties = near[-1:]
        if level < last:
            state = kernel(
                functools.partial(level_kernel, level),
                jax.ShapeDtypeStruct(state.shape, state.dtype),
                [own, other, mixes],
                ties,
                name="level_state",
            )
    return pl.pallas_call(
        functools.partial(tail_kernel, last),
        out_shape=jax.ShapeDtypeStruct((2, columns, panels), jnp.bfloat16),
        in_specs=[in_vmem()] * (4 + len(near)),
        out_specs=anywhere(),
        scratch_shapes=[pltpu.VMEM((2, columns, panels), jnp.bfloat16), pltpu.SemaphoreType.DMA((len(near),))],
        compiler_params=params(),
        cost_estimate=pl.CostEstimate(flops=4 * rows * rank * panels, bytes_accessed=2**21, transcendentals=0),
        name="expand_state",
    )(own, other, mixes, expand, *near)


def solution(mesh):
    return jax.shard_map(
        per_device,
        mesh=mesh,
        in_specs=(
            P(None, None, ("leaf", "sub")),
            P(None, ("leaf", "sub")),
            P(("leaf", "sub")),
            P(("leaf", "sub")),
            P(("leaf", "sub"), None),
            P(("leaf", "sub"), None),
            P(None, None, ("leaf", "sub")),
            P(("leaf", "sub"), None, None, None, None, None),
            P(None, None, ("leaf", "sub")),
        ),
        out_specs=P(None, None, ("leaf", "sub")),
        check_vma=False,
    )
```

```python
import functools
import math

import jax
import jax.numpy as jnp
from jax import lax
from jax.experimental import pallas as pl
from jax.experimental.pallas import tpu as pltpu
from jax.sharding import PartitionSpec as P

HB = 2
PACK = 16

SOFTENING = 0.05
FOUR_PI = 4.0 * math.pi

SIN_COEFFS = (4.442867902822206, -7.307443412968344, 3.5947879989545957, -0.7843738193353357)
COS_COEFFS = (1.4142134965639892, -6.978850988075765, 5.739461166775787, -1.8835629581956719, 0.3106981253821905)

NT = (((1,), (1,)), ((), ()))
NN = (((1,), (0,)), ((), ()))
TN = (((0,), (0,)), ((), ()))

NEAR_PLAN = {5: 2, 6: 2, 7: 2}
FIRST_HALO = 3
SECOND_HALO = 4

VMEM_LIMIT = 16 * 1024 * 1024
WHOLE_VMEM = 63 * 1024 * 1024


def dot(left, right, dims):
    return lax.dot_general(left, right, dims, preferred_element_type=jnp.float32)


def horner(coeffs, x):
    total = coeffs[-1] * x + coeffs[-2]
    for c in reversed(coeffs[:-2]):
        total = total * x + c
    return total


def rows_of(values, rows, count):
    index = lax.broadcasted_iota(jnp.int32, (rows, count), 0)
    total = jnp.zeros((rows, count), jnp.float32)
    for i, value in enumerate(values):
        total = jnp.where(index == i, value, total)
    return total


def head_kernel(skeleton_hbm, density_hbm, compress_hbm, mix, state, first_mix, skeleton, density, compress, sems):
    copies = [
        pltpu.make_async_copy(skeleton_hbm, skeleton, sems.at[0]),
        pltpu.make_async_copy(density_hbm, density, sems.at[1]),
        pltpu.make_async_copy(compress_hbm, compress, sems.at[2]),
        pltpu.make_async_copy(mix.at[0], first_mix, sems.at[3]),
    ]
    for copy in copies:
        copy.start()
    rank = skeleton.shape[1]
    panels = density.shape[1]
    columns = density.shape[0] // 2
    index = lax.broadcasted_iota(jnp.int32, (panels, rank), 0)
    copies[0].wait()
    onehot = (index == skeleton[...]).astype(jnp.float32).astype(jnp.bfloat16)
    copies[1].wait()
    d = density[...]
    picked = dot(d, onehot, NN)
    copies[2].wait()
    product = dot(d, compress[...], NT)
    real = product[:columns, :rank] - product[columns:, rank:] + picked[:columns]
    imag = product[:columns, rank:] + product[columns:, :rank] + picked[columns:]
    for i in range(state.shape[0]):
        state[i, 0] = real.astype(state.dtype)
        state[i, 1] = imag.astype(state.dtype)
    copies[3].wait()


def geometry_rows(coords, weights, count):
    c = coords.astype(jnp.float32)
    w = weights.astype(jnp.float32)
    return rows_of([c[0:1], c[1:2], c[2:3], w], PACK, count).astype(jnp.bfloat16)


def tail_strip_kernel(density, coords, weights, after, geometry, strip):
    del after
    rows, panels = density.shape
    width = strip.shape[1]
    geo = geometry_rows(coords[...], weights[...], panels)
    geometry[...] = geo
    strip[0:rows, :] = density[:, panels - width : panels]
    strip[rows : rows + PACK, :] = geo[:, panels - width : panels]


def head_strip_kernel(density, geometry, after, strip):
    del after
    rows = density.shape[0]
    width = strip.shape[1]
    strip[0:rows, :] = density[:, 0:width]
    strip[rows : rows + PACK, :] = geometry[:, 0:width]


def prepare_kernel(counts, neighbors, geometry, left, right, source, target, factor):
    rows = left.shape[0] - PACK
    panels = geometry.shape[1]
    halo = left.shape[1]
    wide = panels + 2 * halo
    box_count, slot_count = neighbors.shape
    size = panels // box_count

    geo = jnp.concatenate(
        [left[rows : rows + PACK, :], geometry[...], right[rows : rows + PACK, :]], axis=1
    ).astype(jnp.float32)
    x, y, z, w = geo[0:1], geo[1:2], geo[2:3], geo[3:4]
    square = x * x + y * y + z * z

    def split(value):
        one = value.astype(jnp.bfloat16).astype(jnp.float32)
        two = (value - one).astype(jnp.bfloat16).astype(jnp.float32)
        return [one, two, value - one - two]

    ones = jnp.ones_like(x)
    source[...] = rows_of(
        [x, y, z] + split(square + SOFTENING * SOFTENING) + [ones] * 3, PACK, wide
    ).astype(jnp.bfloat16)
    at = slice(halo, halo + panels)
    target[...] = rows_of(
        [-2.0 * x[:, at], -2.0 * y[:, at], -2.0 * z[:, at]] + [ones[:, at]] * 3 + split(square[:, at]),
        PACK,
        panels,
    ).astype(jnp.bfloat16)

    slots = neighbors[...]
    live_count = jnp.zeros((box_count, 1), jnp.int32)
    box_id = lax.broadcasted_iota(jnp.int32, (box_count, 1), 0)
    for b in range(box_count):
        live_count = jnp.where(box_id == b, counts[b], live_count)
    slot_id = lax.broadcasted_iota(jnp.int32, (box_count, slot_count), 1)
    slots = jnp.where(slot_id < live_count, slots, -1)
    for g in range(wide // size):
        times = jnp.sum(jnp.where(slots == g, 1.0 / FOUR_PI, 0.0), axis=1, keepdims=True)
        span = slice(g * size, (g + 1) * size)
        factor[:, span] = times * w[:, span]


def near_kernel(first, density, left, right, source, target, factor, after, out, tiles):
    del after
    rows, panels = density.shape
    columns = rows // 2
    halo = left.shape[1]
    wide = panels + 2 * halo
    size = panels // factor.shape[0]
    chunk = 2 * size

    for i in range(out.shape[2] // size):
        b = first + i
        mine = target[:, b * size : (b + 1) * size]
        for begin in range(0, wide, chunk):
            span = slice(begin, begin + chunk)
            r2 = dot(mine, source[:, span], TN)
            inverse = lax.rsqrt(r2)
            radius = r2 * inverse
            f = radius - jnp.round(radius)
            q = f * f
            u = f * horner(SIN_COEFFS, q)
            v = horner(COS_COEFFS, q)
            a = inverse * factor[b : b + 1, span]
            au = a * u
            tiles[i, 0:size, span] = (a - au * u).astype(jnp.bfloat16)
            tiles[i, size : 2 * size, span] = (au * v).astype(jnp.bfloat16)
        total = dot(density[...], tiles[i, :, halo : halo + panels], NT)
        total += dot(left[0:rows, :], tiles[i, :, 0:halo], NT)
        total += dot(right[0:rows, :], tiles[i, :, halo + panels : wide], NT)
        place = slice(i * size, (i + 1) * size)
        out[0, :, place] = total[:columns, :size] - total[columns:, size:]
        out[1, :, place] = total[:columns, size:] + total[columns:, :size]


def flatten(pair):
    return pair.reshape(2 * pair.shape[1], pair.shape[2])


def add_level(level, own, other, mix):
    columns, rank = own.shape[1:]
    product = dot(flatten(other[...]), flatten(mix[level, 1]), NT)
    real = own[0] + product[:columns, :rank] - product[columns:, rank:]
    imag = own[1] + product[:columns, rank:] + product[columns:, :rank]
    return real.astype(jnp.bfloat16), imag.astype(jnp.bfloat16)


def apply(states, matrices):
    columns, rank = states[0].shape[0] // 2, states[0].shape[1]
    total = dot(states[0], flatten(matrices[0]), NT)
    for state, matrix in zip(states[1:], matrices[1:]):
        total += dot(state, flatten(matrix), NT)
    real = total[:columns, :rank] - total[columns:, rank:]
    imag = total[:columns, rank:] + total[columns:, :rank]
    return jnp.concatenate([real, imag], axis=0).astype(jnp.bfloat16)


def two_level_kernel(gathered, far_mix, mix, *rest):
    out = rest[-1]
    me = lax.axis_index("sub")
    states = [flatten(gathered[me ^ k]) for k in range(4)]
    mine = apply(states[:2], [mix[0, 0], mix[0, 1]])
    partner = apply(states[2:], [far_mix[0], far_mix[1]])
    result = apply([mine, partner], [mix[1, 0], mix[1, 1]])
    columns = out.shape[1]
    out[0] = result[:columns]
    out[1] = result[columns:]


def level_kernel(level, own, other, mix, *rest):
    out = rest[-1]
    out[0], out[1] = add_level(level, own, other, mix)


def tail_kernel(level, own, other, mix, expand, *rest):
    near, (out, block, sems) = rest[:-3], rest[-3:]
    columns = own.shape[1]
    s = jnp.concatenate(add_level(level, own, other, mix), axis=0)
    copies = []
    start = 0
    for i, piece in enumerate(near):
        at = slice(start, start + piece.shape[2])
        start += piece.shape[2]
        first = dot(s, expand[0, :, at], NN)
        second = dot(s, expand[1, :, at], NN)
        real = first[:columns] - second[columns:]
        imag = second[:columns] + first[columns:]
        block[0, :, at] = (real + piece[0]).astype(block.dtype)
        block[1, :, at] = (imag + piece[1]).astype(block.dtype)
        copies.append(pltpu.make_async_copy(block.at[:, :, at], out.at[:, :, at], sems.at[i]))
        copies[-1].start()
    for copy in copies:
        copy.wait()


def params(limit=VMEM_LIMIT):
    return pltpu.CompilerParams(vmem_limit_bytes=limit)


def in_vmem():
    return pl.BlockSpec(memory_space=pltpu.VMEM)


def anywhere():
    return pl.BlockSpec(memory_space=pl.ANY)


def exchange(value, axis, stride):
    mask = 2**stride
    pairs = [(source, source ^ mask) for source in range(lax.axis_size(axis))]
    return lax.ppermute(value, axis, pairs)


def shift(value, step):
    axes = ("leaf", "sub")
    count = lax.axis_size(axes)
    if step > 0:
        pairs = [(i, i + 1) for i in range(count - 1)]
    else:
        pairs = [(i + 1, i) for i in range(count - 1)]
    return lax.ppermute(value, axes, pairs)


def pair_product(left, right):
    columns = left.shape[1]
    rank_rows = right.shape[1]
    product = dot(left.reshape(2 * columns, -1), right.reshape(2 * rank_rows, -1), NT)
    real = product[:columns, :rank_rows] - product[columns:, rank_rows:]
    imag = product[:columns, rank_rows:] + product[columns:, :rank_rows]
    return jnp.stack([real, imag])


def per_device(density, coords, weights, counts, neighbors, skeleton, compress, mix, expand):
    columns, panels = density.shape[1:]
    rank = compress.shape[1]
    box_count = counts.shape[0]
    size = panels // box_count
    halo = HB * size
    rows = 2 * columns
    flat = density.reshape(rows, panels)
    basis = compress.reshape(2 * rank, panels)

    mixes = mix[0]
    copies, first_mix = pl.pallas_call(
        head_kernel,
        out_shape=(
            jax.ShapeDtypeStruct((4, 2, columns, rank), jnp.bfloat16),
            jax.ShapeDtypeStruct(mixes.shape[1:], jnp.bfloat16),
        ),
        in_specs=[pl.BlockSpec(memory_space=pltpu.HBM)] * 4,
        out_specs=(in_vmem(), in_vmem()),
        scratch_shapes=[
            pltpu.VMEM(skeleton.shape, skeleton.dtype),
            pltpu.VMEM(flat.shape, flat.dtype),
            pltpu.VMEM(basis.shape, basis.dtype),
            pltpu.SemaphoreType.DMA((4,)),
        ],
        compiler_params=params(WHOLE_VMEM),
        cost_estimate=pl.CostEstimate(flops=2 * rows * panels * 3 * rank, bytes_accessed=2**20, transcendentals=0),
        name="compress_density",
    )(skeleton, flat, basis, mixes)

    strip = jax.ShapeDtypeStruct((rows + PACK, halo), jnp.bfloat16)
    cheap = pl.CostEstimate(flops=2**20, bytes_accessed=2**18, transcendentals=0)

    def tail_strip(after):
        return pl.pallas_call(
            tail_strip_kernel,
            out_shape=(jax.ShapeDtypeStruct((PACK, panels), jnp.bfloat16), strip),
            in_specs=[in_vmem()] * 3 + [anywhere()],
            out_specs=(in_vmem(),) * 2,
            compiler_params=params(),
            cost_estimate=cheap,
            name="tail_strip",
        )(flat, coords, weights[None, :], after)

    def head_strip(after):
        return pl.pallas_call(
            head_strip_kernel,
            out_shape=strip,
            in_specs=[in_vmem()] * 2 + [anywhere()],
            out_specs=in_vmem(),
            compiler_params=params(),
            cost_estimate=cheap,
            name="head_strip",
        )(flat, geometry, after)

    sub_levels = lax.axis_size("sub").bit_length() - 1
    leaf_levels = lax.axis_size("leaf").bit_length() - 1
    steps = [("sub", i) for i in range(sub_levels)] + [("leaf", i) for i in range(leaf_levels)]
    wide = panels + 2 * halo

    def kernel(body, out_shape, operands, after=(), scratch=(), cost=cheap, name=None):
        one = not isinstance(out_shape, tuple)
        return pl.pallas_call(
            body,
            out_shape=out_shape,
            in_specs=[in_vmem()] * len(operands) + [anywhere()] * len(after),
            out_specs=in_vmem() if one else (in_vmem(),) * len(out_shape),
            scratch_shapes=list(scratch),
            compiler_params=params(),
            cost_estimate=cost,
            name=name,
        )(*operands, *after)

    def prepare():
        return pl.pallas_call(
            prepare_kernel,
            out_shape=(
                jax.ShapeDtypeStruct((PACK, wide), jnp.bfloat16),
                jax.ShapeDtypeStruct((PACK, panels), jnp.bfloat16),
                jax.ShapeDtypeStruct((box_count, wide), jnp.float32),
            ),
            in_specs=[pl.BlockSpec(memory_space=pltpu.SMEM)] + [in_vmem()] * 4,
            out_specs=(in_vmem(),) * 3,
            compiler_params=params(),
            cost_estimate=cheap,
            name="prepare_near",
        )(counts, neighbors, geometry, left, right)

    def near_boxes(first, boxes, after):
        return kernel(
            functools.partial(near_kernel, first),
            jax.ShapeDtypeStruct((2, columns, boxes * size), jnp.float32),
            [flat, left, right, source, target, factor],
            [after],
            [pltpu.VMEM((boxes, 2 * size, wide), jnp.bfloat16)],
            pl.CostEstimate(
                flops=2 * boxes * rows * wide * 2 * size, bytes_accessed=2**21, transcendentals=boxes * size * wide
            ),
            "near_boxes",
        )

    near = []
    done = 0
    last = len(steps) - 1
    far_mix = exchange(first_mix, *steps[1])
    gathered = lax.all_to_all(copies, "sub", 0, 0)
    state = kernel(
        two_level_kernel,
        jax.ShapeDtypeStruct((2, columns, rank), jnp.bfloat16),
        [gathered, far_mix, mixes],
        name="levels_0_1",
    )
    for level, (axis, stride) in list(enumerate(steps))[2:]:
        other = exchange(state, axis, stride)
        own = pair_product(state, mixes[level, 0])
        ties = []
        if level == min(FIRST_HALO, last):
            geometry, strip_out = tail_strip(state)
            left = shift(strip_out, 1)
        if level == min(SECOND_HALO, last):
            right = shift(head_strip(state), -1)
        boxes = box_count - done if level == last else NEAR_PLAN.get(level, 0)
        if boxes:
            if not near:
                source, target, factor = prepare()
            near.append(near_boxes(done, boxes, state))
            done += boxes
            ties = near[-1:]
        if level < last:
            state = kernel(
                functools.partial(level_kernel, level),
                jax.ShapeDtypeStruct(state.shape, state.dtype),
                [own, other, mixes],
                ties,
                name="level_state",
            )
    return pl.pallas_call(
        functools.partial(tail_kernel, last),
        out_shape=jax.ShapeDtypeStruct((2, columns, panels), jnp.bfloat16),
        in_specs=[in_vmem()] * (4 + len(near)),
        out_specs=anywhere(),
        scratch_shapes=[pltpu.VMEM((2, columns, panels), jnp.bfloat16), pltpu.SemaphoreType.DMA((len(near),))],
        compiler_params=params(),
        cost_estimate=pl.CostEstimate(flops=4 * rows * rank * panels, bytes_accessed=2**21, transcendentals=0),
        name="expand_state",
    )(own, other, mixes, expand, *near)


def solution(mesh):
    return jax.shard_map(
        per_device,
        mesh=mesh,
        in_specs=(
            P(None, None, ("leaf", "sub")),
            P(None, ("leaf", "sub")),
            P(("leaf", "sub")),
            P(("leaf", "sub")),
            P(("leaf", "sub"), None),
            P(("leaf", "sub"), None),
            P(None, None, ("leaf", "sub")),
            P(("leaf", "sub"), None, None, None, None, None),
            P(None, None, ("leaf", "sub")),
        ),
        out_specs=P(None, None, ("leaf", "sub")),
        check_vma=False,
    )
```

```python
import functools
import math

import jax
import jax.numpy as jnp
from jax import lax
from jax.experimental import pallas as pl
from jax.experimental.pallas import tpu as pltpu
from jax.sharding import PartitionSpec as P

HB = 2
PACK = 16

SOFTENING = 0.05
FOUR_PI = 4.0 * math.pi

SIN_COEFFS = (4.442867902822206, -7.307443412968344, 3.5947879989545957, -0.7843738193353357)
COS_COEFFS = (1.4142134965639892, -6.978850988075765, 5.739461166775787, -1.8835629581956719, 0.3106981253821905)

NT = (((1,), (1,)), ((), ()))
NN = (((1,), (0,)), ((), ()))
TN = (((0,), (0,)), ((), ()))

NEAR_PLAN = {6: 2, 7: 3}
FIRST_HALO = 3
SECOND_HALO = 5

VMEM_LIMIT = 16 * 1024 * 1024
WHOLE_VMEM = 63 * 1024 * 1024


def dot(left, right, dims):
    return lax.dot_general(left, right, dims, preferred_element_type=jnp.float32)


def horner(coeffs, x):
    total = coeffs[-1] * x + coeffs[-2]
    for c in reversed(coeffs[:-2]):
        total = total * x + c
    return total


def rows_of(values, rows, count):
    index = lax.broadcasted_iota(jnp.int32, (rows, count), 0)
    total = jnp.zeros((rows, count), jnp.float32)
    for i, value in enumerate(values):
        total = jnp.where(index == i, value, total)
    return total


def head_kernel(skeleton_hbm, density_hbm, compress_hbm, mix, state, first_mix, skeleton, density, compress, sems):
    copies = [
        pltpu.make_async_copy(skeleton_hbm, skeleton, sems.at[0]),
        pltpu.make_async_copy(density_hbm, density, sems.at[1]),
        pltpu.make_async_copy(compress_hbm, compress, sems.at[2]),
        pltpu.make_async_copy(mix.at[0], first_mix, sems.at[3]),
    ]
    for copy in copies:
        copy.start()
    rank = skeleton.shape[1]
    panels = density.shape[1]
    columns = density.shape[0] // 2
    index = lax.broadcasted_iota(jnp.int32, (panels, rank), 0)
    copies[0].wait()
    onehot = (index == skeleton[...]).astype(jnp.float32).astype(jnp.bfloat16)
    copies[1].wait()
    d = density[...]
    picked = dot(d, onehot, NN)
    copies[2].wait()
    product = dot(d, compress[...], NT)
    real = product[:columns, :rank] - product[columns:, rank:] + picked[:columns]
    imag = product[:columns, rank:] + product[columns:, :rank] + picked[columns:]
    for i in range(state.shape[0]):
        state[i, 0] = real.astype(state.dtype)
        state[i, 1] = imag.astype(state.dtype)
    copies[3].wait()


def geometry_rows(coords, weights, count):
    c = coords.astype(jnp.float32)
    w = weights.astype(jnp.float32)
    return rows_of([c[0:1], c[1:2], c[2:3], w], PACK, count).astype(jnp.bfloat16)


def tail_strip_kernel(density, coords, weights, after, geometry, strip):
    del after
    rows, panels = density.shape
    width = strip.shape[1]
    geo = geometry_rows(coords[...], weights[...], panels)
    geometry[...] = geo
    strip[0:rows, :] = density[:, panels - width : panels]
    strip[rows : rows + PACK, :] = geo[:, panels - width : panels]


def head_strip_kernel(density, geometry, after, strip):
    del after
    rows = density.shape[0]
    width = strip.shape[1]
    strip[0:rows, :] = density[:, 0:width]
    strip[rows : rows + PACK, :] = geometry[:, 0:width]


def prepare_kernel(counts, neighbors, geometry, left, right, source, target, factor):
    rows = left.shape[0] - PACK
    panels = geometry.shape[1]
    halo = left.shape[1]
    wide = panels + 2 * halo
    box_count, slot_count = neighbors.shape
    size = panels // box_count

    geo = jnp.concatenate(
        [left[rows : rows + PACK, :], geometry[...], right[rows : rows + PACK, :]], axis=1
    ).astype(jnp.float32)
    x, y, z, w = geo[0:1], geo[1:2], geo[2:3], geo[3:4]
    square = x * x + y * y + z * z

    def split(value):
        one = value.astype(jnp.bfloat16).astype(jnp.float32)
        two = (value - one).astype(jnp.bfloat16).astype(jnp.float32)
        return [one, two, value - one - two]

    ones = jnp.ones_like(x)
    source[...] = rows_of(
        [x, y, z] + split(square + SOFTENING * SOFTENING) + [ones] * 3, PACK, wide
    ).astype(jnp.bfloat16)
    at = slice(halo, halo + panels)
    target[...] = rows_of(
        [-2.0 * x[:, at], -2.0 * y[:, at], -2.0 * z[:, at]] + [ones[:, at]] * 3 + split(square[:, at]),
        PACK,
        panels,
    ).astype(jnp.bfloat16)

    slots = neighbors[...]
    live_count = jnp.zeros((box_count, 1), jnp.int32)
    box_id = lax.broadcasted_iota(jnp.int32, (box_count, 1), 0)
    for b in range(box_count):
        live_count = jnp.where(box_id == b, counts[b], live_count)
    slot_id = lax.broadcasted_iota(jnp.int32, (box_count, slot_count), 1)
    slots = jnp.where(slot_id < live_count, slots, -1)
    for g in range(wide // size):
        times = jnp.sum(jnp.where(slots == g, 1.0 / FOUR_PI, 0.0), axis=1, keepdims=True)
        span = slice(g * size, (g + 1) * size)
        factor[:, span] = times * w[:, span]


def near_kernel(first, density, left, right, source, target, factor, after, out, tiles):
    del after
    rows, panels = density.shape
    columns = rows // 2
    halo = left.shape[1]
    wide = panels + 2 * halo
    size = panels // factor.shape[0]
    chunk = 2 * size

    for i in range(out.shape[2] // size):
        b = first + i
        mine = target[:, b * size : (b + 1) * size]
        for begin in range(0, wide, chunk):
            span = slice(begin, begin + chunk)
            r2 = dot(mine, source[:, span], TN)
            inverse = lax.rsqrt(r2)
            radius = r2 * inverse
            f = radius - jnp.round(radius)
            q = f * f
            u = f * horner(SIN_COEFFS, q)
            v = horner(COS_COEFFS, q)
            a = inverse * factor[b : b + 1, span]
            au = a * u
            tiles[i, 0:size, span] = (a - au * u).astype(jnp.bfloat16)
            tiles[i, size : 2 * size, span] = (au * v).astype(jnp.bfloat16)
        total = dot(density[...], tiles[i, :, halo : halo + panels], NT)
        total += dot(left[0:rows, :], tiles[i, :, 0:halo], NT)
        total += dot(right[0:rows, :], tiles[i, :, halo + panels : wide], NT)
        place = slice(i * size, (i + 1) * size)
        out[0, :, place] = total[:columns, :size] - total[columns:, size:]
        out[1, :, place] = total[:columns, size:] + total[columns:, :size]


def flatten(pair):
    return pair.reshape(2 * pair.shape[1], pair.shape[2])


def add_level(level, own, other, mix):
    columns, rank = own.shape[1:]
    product = dot(flatten(other[...]), flatten(mix[level, 1]), NT)
    real = own[0] + product[:columns, :rank] - product[columns:, rank:]
    imag = own[1] + product[:columns, rank:] + product[columns:, :rank]
    return real.astype(jnp.bfloat16), imag.astype(jnp.bfloat16)


def apply(states, matrices):
    columns, rank = states[0].shape[0] // 2, states[0].shape[1]
    total = dot(states[0], flatten(matrices[0]), NT)
    for state, matrix in zip(states[1:], matrices[1:]):
        total += dot(state, flatten(matrix), NT)
    real = total[:columns, :rank] - total[columns:, rank:]
    imag = total[:columns, rank:] + total[columns:, :rank]
    return jnp.concatenate([real, imag], axis=0).astype(jnp.bfloat16)


def two_level_kernel(gathered, far_mix, mix, *rest):
    out = rest[-1]
    me = lax.axis_index("sub")
    states = [flatten(gathered[me ^ k]) for k in range(4)]
    mine = apply(states[:2], [mix[0, 0], mix[0, 1]])
    partner = apply(states[2:], [far_mix[0], far_mix[1]])
    result = apply([mine, partner], [mix[1, 0], mix[1, 1]])
    columns = out.shape[1]
    out[0] = result[:columns]
    out[1] = result[columns:]


def level_kernel(level, own, other, mix, *rest):
    out = rest[-1]
    out[0], out[1] = add_level(level, own, other, mix)


def tail_kernel(level, own, other, mix, expand, *rest):
    near, (out, block, sems) = rest[:-3], rest[-3:]
    columns = own.shape[1]
    s = jnp.concatenate(add_level(level, own, other, mix), axis=0)
    copies = []
    start = 0
    for i, piece in enumerate(near):
        at = slice(start, start + piece.shape[2])
        start += piece.shape[2]
        first = dot(s, expand[0, :, at], NN)
        second = dot(s, expand[1, :, at], NN)
        real = first[:columns] - second[columns:]
        imag = second[:columns] + first[columns:]
        block[0, :, at] = (real + piece[0]).astype(block.dtype)
        block[1, :, at] = (imag + piece[1]).astype(block.dtype)
        copies.append(pltpu.make_async_copy(block.at[:, :, at], out.at[:, :, at], sems.at[i]))
        copies[-1].start()
    for copy in copies:
        copy.wait()


def params(limit=VMEM_LIMIT):
    return pltpu.CompilerParams(vmem_limit_bytes=limit)


def in_vmem():
    return pl.BlockSpec(memory_space=pltpu.VMEM)


def anywhere():
    return pl.BlockSpec(memory_space=pl.ANY)


def exchange(value, axis, stride):
    mask = 2**stride
    pairs = [(source, source ^ mask) for source in range(lax.axis_size(axis))]
    return lax.ppermute(value, axis, pairs)


def shift(value, step):
    axes = ("leaf", "sub")
    count = lax.axis_size(axes)
    if step > 0:
        pairs = [(i, i + 1) for i in range(count - 1)]
    else:
        pairs = [(i + 1, i) for i in range(count - 1)]
    return lax.ppermute(value, axes, pairs)


def pair_product(left, right):
    columns = left.shape[1]
    rank_rows = right.shape[1]
    product = dot(left.reshape(2 * columns, -1), right.reshape(2 * rank_rows, -1), NT)
    real = product[:columns, :rank_rows] - product[columns:, rank_rows:]
    imag = product[:columns, rank_rows:] + product[columns:, :rank_rows]
    return jnp.stack([real, imag])


def per_device(density, coords, weights, counts, neighbors, skeleton, compress, mix, expand):
    columns, panels = density.shape[1:]
    rank = compress.shape[1]
    box_count = counts.shape[0]
    size = panels // box_count
    halo = HB * size
    rows = 2 * columns
    flat = density.reshape(rows, panels)
    basis = compress.reshape(2 * rank, panels)

    mixes = mix[0]
    copies, first_mix = pl.pallas_call(
        head_kernel,
        out_shape=(
            jax.ShapeDtypeStruct((4, 2, columns, rank), jnp.bfloat16),
            jax.ShapeDtypeStruct(mixes.shape[1:], jnp.bfloat16),
        ),
        in_specs=[pl.BlockSpec(memory_space=pltpu.HBM)] * 4,
        out_specs=(in_vmem(), in_vmem()),
        scratch_shapes=[
            pltpu.VMEM(skeleton.shape, skeleton.dtype),
            pltpu.VMEM(flat.shape, flat.dtype),
            pltpu.VMEM(basis.shape, basis.dtype),
            pltpu.SemaphoreType.DMA((4,)),
        ],
        compiler_params=params(WHOLE_VMEM),
        cost_estimate=pl.CostEstimate(flops=2 * rows * panels * 3 * rank, bytes_accessed=2**20, transcendentals=0),
        name="compress_density",
    )(skeleton, flat, basis, mixes)

    strip = jax.ShapeDtypeStruct((rows + PACK, halo), jnp.bfloat16)
    cheap = pl.CostEstimate(flops=2**20, bytes_accessed=2**18, transcendentals=0)

    def tail_strip(after):
        return pl.pallas_call(
            tail_strip_kernel,
            out_shape=(jax.ShapeDtypeStruct((PACK, panels), jnp.bfloat16), strip),
            in_specs=[in_vmem()] * 3 + [anywhere()],
            out_specs=(in_vmem(),) * 2,
            compiler_params=params(),
            cost_estimate=cheap,
            name="tail_strip",
        )(flat, coords, weights[None, :], after)

    def head_strip(after):
        return pl.pallas_call(
            head_strip_kernel,
            out_shape=strip,
            in_specs=[in_vmem()] * 2 + [anywhere()],
            out_specs=in_vmem(),
            compiler_params=params(),
            cost_estimate=cheap,
            name="head_strip",
        )(flat, geometry, after)

    sub_levels = lax.axis_size("sub").bit_length() - 1
    leaf_levels = lax.axis_size("leaf").bit_length() - 1
    steps = [("sub", i) for i in range(sub_levels)] + [("leaf", i) for i in range(leaf_levels)]
    wide = panels + 2 * halo

    def kernel(body, out_shape, operands, after=(), scratch=(), cost=cheap, name=None):
        one = not isinstance(out_shape, tuple)
        return pl.pallas_call(
            body,
            out_shape=out_shape,
            in_specs=[in_vmem()] * len(operands) + [anywhere()] * len(after),
            out_specs=in_vmem() if one else (in_vmem(),) * len(out_shape),
            scratch_shapes=list(scratch),
            compiler_params=params(),
            cost_estimate=cost,
            name=name,
        )(*operands, *after)

    def prepare():
        return pl.pallas_call(
            prepare_kernel,
            out_shape=(
                jax.ShapeDtypeStruct((PACK, wide), jnp.bfloat16),
                jax.ShapeDtypeStruct((PACK, panels), jnp.bfloat16),
                jax.ShapeDtypeStruct((box_count, wide), jnp.float32),
            ),
            in_specs=[pl.BlockSpec(memory_space=pltpu.SMEM)] + [in_vmem()] * 4,
            out_specs=(in_vmem(),) * 3,
            compiler_params=params(),
            cost_estimate=cheap,
            name="prepare_near",
        )(counts, neighbors, geometry, left, right)

    def near_boxes(first, boxes, after):
        return kernel(
            functools.partial(near_kernel, first),
            jax.ShapeDtypeStruct((2, columns, boxes * size), jnp.float32),
            [flat, left, right, source, target, factor],
            [after],
            [pltpu.VMEM((boxes, 2 * size, wide), jnp.bfloat16)],
            pl.CostEstimate(
                flops=2 * boxes * rows * wide * 2 * size, bytes_accessed=2**21, transcendentals=boxes * size * wide
            ),
            "near_boxes",
        )

    near = []
    done = 0
    last = len(steps) - 1
    far_mix = exchange(first_mix, *steps[1])
    gathered = lax.all_to_all(copies, "sub", 0, 0)
    state = kernel(
        two_level_kernel,
        jax.ShapeDtypeStruct((2, columns, rank), jnp.bfloat16),
        [gathered, far_mix, mixes],
        name="levels_0_1",
    )
    for level, (axis, stride) in list(enumerate(steps))[2:]:
        other = exchange(state, axis, stride)
        own = pair_product(state, mixes[level, 0])
        ties = []
        if level == min(FIRST_HALO, last):
            geometry, strip_out = tail_strip(state)
            left = shift(strip_out, 1)
        if level == min(SECOND_HALO, last):
            right = shift(head_strip(state), -1)
        boxes = box_count - done if level == last else NEAR_PLAN.get(level, 0)
        if boxes:
            if not near:
                source, target, factor = prepare()
            near.append(near_boxes(done, boxes, state))
            done += boxes
            ties = near[-1:]
        if level < last:
            state = kernel(
                functools.partial(level_kernel, level),
                jax.ShapeDtypeStruct(state.shape, state.dtype),
                [own, other, mixes],
                ties,
                name="level_state",
            )
    return pl.pallas_call(
        functools.partial(tail_kernel, last),
        out_shape=jax.ShapeDtypeStruct((2, columns, panels), jnp.bfloat16),
        in_specs=[in_vmem()] * (4 + len(near)),
        out_specs=anywhere(),
        scratch_shapes=[pltpu.VMEM((2, columns, panels), jnp.bfloat16), pltpu.SemaphoreType.DMA((len(near),))],
        compiler_params=params(),
        cost_estimate=pl.CostEstimate(flops=4 * rows * rank * panels, bytes_accessed=2**21, transcendentals=0),
        name="expand_state",
    )(own, other, mixes, expand, *near)


def solution(mesh):
    return jax.shard_map(
        per_device,
        mesh=mesh,
        in_specs=(
            P(None, None, ("leaf", "sub")),
            P(None, ("leaf", "sub")),
            P(("leaf", "sub")),
            P(("leaf", "sub")),
            P(("leaf", "sub"), None),
            P(("leaf", "sub"), None),
            P(None, None, ("leaf", "sub")),
            P(("leaf", "sub"), None, None, None, None, None),
            P(None, None, ("leaf", "sub")),
        ),
        out_specs=P(None, None, ("leaf", "sub")),
        check_vma=False,
    )
```
